128 devices in a mesh: pts: 32 (over y_hi, x, z), lev: 4 (over y_lo, core).
Axes of the slice: x: 4, y: 4 (y_hi: 2, y_lo: 2; y = y_hi * 2 + y_lo), z: 4, core: 2. Of those that a mesh axis runs over, the one named last changes fastest.
Arguments:
- members: bfloat16 [64, 32, 262144], P('pts', 'lev'), may hold values from -6 to 6
- gradient: float32 [32, 262144], P('lev', 'pts'), may hold values from -0.6 to 0.6
- horiz_loc: bfloat16 [32768, 128, 128], P(('pts', 'lev')), may hold values from 0 to 1
- vert_loc: bfloat16 [32768, 8, 128], P(('pts', 'lev')), may hold values from 0 to 1
- tile_block: int32 [32768], P(('pts', 'lev')), may hold values from 0 to 63
- tile_obs: int32 [32768], P(('pts', 'lev')), may hold values from 0 to 127, as said below
- tile_live: int32 [128], P(('pts', 'lev')), may hold values from 2 to 256, as said below
- obs_pert: bfloat16 [64, 16384], P(None, ('pts', 'lev')), may hold values from -6 to 6
- innovation: float32 [16384], P(('pts', 'lev')), may hold values from -6 to 6
- obs_error: float32 [16384], P(('pts', 'lev')), may hold values from 0.5 to 2
- obs_count: int32 [128], P(('pts', 'lev')), may hold values from 1 to 128, as said below
Outputs:
- sensitivity: float32 [16384], P(('pts', 'lev'))
- impact: float32 [16384], P(('pts', 'lev'))
The draws below stay inside these ranges and needn't reach their ends.
Inputs may be any that keep to these rules, and one draw needn't show every extreme that they name: `tile_obs`: the device that owns observation block b is b // 1 in pts-major order; for every tile slot its pts index lies within 2 of the pts index of the slot's device, counted cyclically; every device's first two slots lie at the offsets 2 and minus 2. `tile_live`: slots of a device at positions below its count are live, the others are ignored; some device has all 256 live. `obs_count`: the live observations of a block are its first ones; some block is full.
All inputs are finite; a program needn't handle non-finite values.
Results may differ from the reference program's by a relative error of at most 0.0029.
Values may be sent and summed in bfloat16 or wider, within the bound.
A program may use at most 384 MiB of HBM per device.

```python
import math
import jax
import jax.numpy as jnp
from jax import lax

K = 64
LEVS = 32
TILE = 128
REACH = 2
CD = 8192
TPD = 256
OBD = 1
LD = 8
COLS = 262144
TILES = 32768
OBLOCKS = 128
OBS = 16384
N_PTS = 32
N_LEV = 4
DEVICES = 128


def draw_tile_obs(key, part):
    key = jax.random.fold_in(key, 11)
    subkeys = jax.random.split(key, 3)
    slot_ids = jnp.arange(TILES, dtype=jnp.int32)
    device = slot_ids // TPD
    home_pts = device // N_LEV
    offset = jax.random.randint(subkeys[0], (TILES,), -REACH, REACH + 1)
    within_dev = slot_ids % TPD
    spread_offset = within_dev - REACH - 1
    offset = jnp.where(within_dev <= 2 * REACH, spread_offset, offset)
    offset = jnp.where(within_dev == 0, REACH, jnp.where(within_dev == 1, -REACH, offset))
    owner_pts = (home_pts + offset) % N_PTS
    owner_lev = jax.random.randint(subkeys[1], (TILES,), 0, N_LEV)
    inner_block = jax.random.randint(subkeys[2], (TILES,), 0, OBD)
    return ((owner_pts * N_LEV + owner_lev) * OBD + inner_block).astype(jnp.int32)


def draw_tile_live(key, part):
    key = jax.random.fold_in(key, 23)
    subkeys = jax.random.split(key, 2)
    counts = jax.random.randint(subkeys[0], (DEVICES,), 2, TPD + 1)
    chosen_dev = jax.random.randint(subkeys[1], (), 0, DEVICES)
    counts = jnp.where(jnp.arange(DEVICES, dtype=jnp.int32) == chosen_dev, TPD, counts)
    return counts.astype(jnp.int32)


def draw_obs_count(key, part):
    key = jax.random.fold_in(key, 37)
    subkeys = jax.random.split(key, 2)
    counts = jax.random.randint(subkeys[0], (OBLOCKS,), 1, TILE + 1)
    chosen_block = jax.random.randint(subkeys[1], (), 0, OBLOCKS)
    counts = jnp.where(jnp.arange(OBLOCKS, dtype=jnp.int32) == chosen_block, TILE, counts)
    return counts.astype(jnp.int32)


def set_ends(values, rng, least, largest):
    longest = values.shape.index(max(values.shape))
    spots = []
    for shift in (0, 1):
        where = [jax.random.randint(jax.random.fold_in(rng, axis), (), 0, length) for axis, length in enumerate(values.shape)]
        where[longest] = (where[longest] + shift) % values.shape[longest]
        spots.append(tuple(where))
    return values.at[spots[0]].set(least).at[spots[1]].set(largest)


def level_of(stream_key, shape, pieces, least, top_value):
    loudness = 1.0
    for dim, parts in pieces:
        draws = jax.random.uniform(jax.random.fold_in(jax.random.fold_in(stream_key, 6), dim), (parts,), jnp.float32, least / len(pieces), top_value / len(pieces))
        loudness = loudness * jnp.repeat(jnp.exp(draws), shape[dim] // parts).reshape((-1,) + (1,) * (len(shape) - 1 - dim))
    return loudness


def centred(stream_key, extent, scale, limit, pieces=(), kind=jnp.bfloat16):
    result = jax.random.normal(stream_key, extent, jnp.float32) * scale
    if len(pieces) > 0:
        result = level_of(stream_key, extent, pieces, -0.22, 0.18) * result
    return jnp.clip(result, min=-limit, max=limit).astype(kind)


def setup_inputs(seed: int = 0) -> dict:
    arg_keys = jax.random.split(jax.random.key(seed), 12)
    return {
        "members": centred(arg_keys[0], (K, LEVS, COLS), 1.0, 6.0, ((0, 32), (1, 4))),
        "gradient": centred(arg_keys[1], (LEVS, COLS), 0.1, 0.6, ((0, 4), (1, 32)), jnp.float32),
        "horiz_loc": jnp.clip(1.0 * jax.random.uniform(arg_keys[2], (TILES, TILE, TILE), jnp.float32) ** level_of(arg_keys[2], (TILES, TILE, TILE), ((0, 128),), -0.2, 0.2), 0.0, 1.0).astype(jnp.bfloat16),
        "vert_loc": jnp.clip(1.0 * jax.random.uniform(arg_keys[3], (TILES, LD, TILE), jnp.float32) ** level_of(arg_keys[3], (TILES, LD, TILE), ((0, 128),), -0.2, 0.2), 0.0, 1.0).astype(jnp.bfloat16),
        "tile_block": set_ends(jax.random.randint(arg_keys[4], (TILES,), 0, CD // TILE), jax.random.fold_in(arg_keys[4], 1), 0, (CD // TILE) - 1).astype(jnp.int32),
        "tile_obs": draw_tile_obs(jax.random.fold_in(arg_keys[11], 71), 0),
        "tile_live": draw_tile_live(jax.random.fold_in(arg_keys[11], 71), 0),
        "obs_pert": centred(arg_keys[7], (K, OBS), 1.0, 6.0, ((1, 128),)),
        "innovation": centred(arg_keys[8], (OBS,), 1.0, 6.0, ((0, 128),), jnp.float32),
        "obs_error": jnp.clip(jnp.exp(math.log(2.0) - 1.3862944 * jax.random.uniform(arg_keys[9], (OBS,), jnp.float32) ** level_of(arg_keys[9], (OBS,), ((0, 128),), -0.2, 0.2)), 0.5, 2.0),
        "obs_count": draw_obs_count(jax.random.fold_in(arg_keys[11], 71), 0),
    }


def reference(members, gradient, horiz_loc, vert_loc, tile_block, tile_obs, tile_live, obs_pert, innovation, obs_error, obs_count):
    device_total = N_PTS * N_LEV
    highest = lax.Precision.HIGHEST

    def device_step(accum, device):
        pts_index = (device // N_LEV).astype(jnp.int32)
        lev_index = (device % N_LEV).astype(jnp.int32)
        zero_index = jnp.int32(0)
        member_part = lax.dynamic_slice(members, (zero_index, lev_index * LD, pts_index * CD), (K, LD, CD))
        grad_part = lax.dynamic_slice(gradient, (lev_index * LD, pts_index * CD), (LD, CD))
        perturbed = (member_part.astype(jnp.float32) * grad_part).astype(jnp.bfloat16)
        first_slot = (device * TPD).astype(jnp.int32)
        horiz = lax.dynamic_slice_in_dim(horiz_loc, first_slot, TPD, 0)
        vert = lax.dynamic_slice_in_dim(vert_loc, first_slot, TPD, 0)
        blocks = lax.dynamic_slice_in_dim(tile_block, first_slot, TPD, 0)
        owners = lax.dynamic_slice_in_dim(tile_obs, first_slot, TPD, 0)
        blocked = perturbed.reshape(K, LD, CD // TILE, TILE)
        chosen = jnp.take(blocked, blocks, axis=2)
        scores = jnp.einsum("kltc,toc->tklo", chosen.astype(jnp.float32), horiz.astype(jnp.float32), precision=highest)
        partial_value = jnp.sum(scores * vert.astype(jnp.float32)[:, None, :, :], axis=2)
        live = jnp.arange(TPD, dtype=jnp.int32) < tile_live[device]
        partial_value = jnp.where(live[:, None, None], partial_value, jnp.zeros_like(partial_value))
        accum = accum + jax.ops.segment_sum(partial_value, owners, num_segments=OBLOCKS)
        return accum, None

    start_accum = jnp.zeros((OBLOCKS, K, TILE), jnp.float32)
    weights, unused = lax.scan(device_step, start_accum, jnp.arange(device_total, dtype=jnp.int32))
    pert_blocks = obs_pert.astype(jnp.float32).reshape(K, OBLOCKS, TILE)
    raw_sum = jnp.einsum("kbo,bko->bo", pert_blocks, weights, precision=highest)
    sens_blocks = raw_sum / (K - 1)
    live_obs = jnp.arange(TILE, dtype=jnp.int32)[None, :] < obs_count[:, None]
    sens_blocks = jnp.where(live_obs, sens_blocks, jnp.zeros_like(sens_blocks))
    sensitivity = sens_blocks.reshape(OBS)
    impact = innovation * sensitivity / obs_error
    return sensitivity, impact
```

```python
import functools

import jax
import jax.numpy as jnp
from jax import lax
from jax.experimental import pallas as pl
from jax.experimental.pallas import tpu as pltpu
from jax.sharding import PartitionSpec as P

MESH = pl.DeviceIdType.MESH
REACH = 2
N_PTS = 32
N_LEV = 4
SIZE = {"y": 2, "x": 4, "z": 4}
NAMES = ("y", "x", "z")
PARTS = ((0, 11), (11, 22), (22, 32))
WIDEST = 11
ORDERS = (("x", "z", "y"), ("z", "y", "x"), ("y", "x", "z"))
UNITS = tuple((k, a, b) for k in (0, 1) for a in (0, 1) for b in (0, 1))
LAG = 2
TILES = 256
GROUP = 16
SLOTS = 32


def distances(unit, axis):
    k, a, b = unit
    return {"y": (0, 1), "x": (a, a + 2), "z": (b, b + 2)}[axis]


def moves():
    count = 0
    for u, unit in enumerate(UNITS):
        for part in range(len(PARTS)):
            held = 1
            for axis in ORDERS[(part + u) % 3]:
                count += held * sum(1 for step in distances(unit, axis) if step)
                held *= 2
    return count


NEAR = [(o, r) for o in range(-REACH, REACH + 1) for r in range(N_LEV) if (o, r) != (0, 0)]


def kernel(
    members, gradient, horiz, vert, block_ref, owner_ref, live_ref, pert,
    out_ref,
    hop1, hop2, hop3, own, grad, tiles, vert_raw, vert_f, scaled, total,
    pert_raw, pert_f, pert_u, marks, select, rows, arrived,
    send_sem, recv_sem, near_send, near_recv, back_send, back_recv, local_sem,
):
    f32, bf16 = jnp.float32, jnp.bfloat16
    me, lev = lax.axis_index("pts"), lax.axis_index("lev")
    here = {"y": me // 16, "x": (me // 4) % 4, "z": me % 4}
    my_slot = (me * N_LEV + lev) % SLOTS

    def place(at):
        return at["y"] * 16 + at["x"] * 4 + at["z"]

    def moved(axis, step):
        at = dict(here)
        at[axis] = (at[axis] + step) % SIZE[axis]
        return place(at)

    local_copies = [
        pltpu.make_async_copy(horiz, tiles, local_sem.at[0]),
        pltpu.make_async_copy(gradient, grad, local_sem.at[1]),
        pltpu.make_async_copy(vert, vert_raw, local_sem.at[2]),
        pltpu.make_async_copy(pert, pert_raw.at[my_slot], local_sem.at[3]),
        pltpu.make_async_copy(
            members.at[:, here["y"], here["x"] // 2, here["x"] % 2, here["z"] // 2, here["z"] % 2],
            own,
            local_sem.at[4],
        ),
    ]

    barrier = pltpu.get_barrier_semaphore()
    line = [("x", 1), ("x", 2), ("x", 3), ("z", 1), ("z", 2), ("z", 3), ("y", 1)]
    for axis, step in line:
        pl.semaphore_signal(barrier, inc=1, device_id={"pts": moved(axis, step)}, device_id_type=MESH)
    near = [((me + o + N_PTS) % N_PTS, (lev + r) % N_LEV) for o, r in NEAR]
    for to in near:
        pl.semaphore_signal(barrier, inc=1, device_id=to, device_id_type=MESH)
    for copy in local_copies:
        copy.start()
    pl.semaphore_wait(barrier, len(line) + len(near))

    near_copies = []
    for i, to in enumerate(near):
        near_copies.append(
            pltpu.make_async_remote_copy(
                src_ref=pert,
                dst_ref=pert_raw.at[my_slot],
                send_sem=near_send.at[i],
                recv_sem=near_recv.at[i],
                device_id=to,
                device_id_type=MESH,
            )
        )

    hops = (hop1, hop2, hop3)
    held = {}
    sent = []

    def begin(u):
        k, a, b = UNITS[u]
        for part, (low, high) in enumerate(PARTS):
            base = members.at[
                k, :, :, (here["x"] + a) % 2, :, (here["z"] + b) % 2, pl.ds(low, high - low)
            ]
            held[u, part] = [({}, base, NAMES, None)]

    def settle(entry):
        if entry is not None and not entry[1]:
            entry[0].wait_recv()
            entry[1] = True

    def advance(u, part, stage, tick):
        low, high = PARTS[part]
        axis = ORDERS[(part + u) % 3][stage]
        fresh, slot = [], 0
        for moved_by, ref, left, entry in held[u, part]:
            settle(entry)
            for step in distances(UNITS[u], axis):
                target = (here[axis] + step) % SIZE[axis]
                index = target if axis == "y" else target // 2
                source = ref.at[tuple(index if n == axis else slice(None) for n in left)]
                rest = tuple(n for n in left if n != axis)
                by = {**moved_by, axis: step}
                if step == 0:
                    fresh.append((by, source, rest, entry))
                    continue
                there = hops[stage].at[
                    (u, part, slot) + (slice(None),) * len(rest) + (pl.ds(0, high - low),)
                ]
                copy = pltpu.make_async_remote_copy(
                    src_ref=source,
                    dst_ref=there,
                    send_sem=send_sem.at[len(sent)],
                    recv_sem=recv_sem.at[len(sent)],
                    device_id={"pts": moved(axis, step)},
                    device_id_type=MESH,
                )
                copy.start()
                sent.append((tick, copy))
                fresh.append((by, there, rest, [copy, False]))
                slot += 1
        held[u, part] = fresh


    def ready_local():
        for copy in local_copies:
            copy.wait()

    def turn_tiles(low, high):
        def body(i, carry):
            turned = [tiles[i * 4 + j].T for j in range(4)]
            for j in range(4):
                tiles[i * 4 + j] = turned[j]
            return carry

        lax.fori_loop(low // 4, high // 4, body, 0)

    def spread_vert():
        def body(i, carry):
            both = vert_raw[i].astype(f32)
            vert_f[2 * i] = both[:8]
            vert_f[2 * i + 1] = both[8:]
            return carry

        lax.fori_loop(0, TILES // 2, body, 0, unroll=4)

    def mark_owners(low, high):
        lanes = lax.broadcasted_iota(jnp.int32, (8, 128), 1)
        live = live_ref[0]

        def body(t, carry):
            slot = owner_ref[t] % SLOTS
            slot = jnp.where(t < live, slot, -1)
            marks[t] = jnp.where(lanes == slot, 1.0, 0.0).astype(f32)
            return carry

        lax.fori_loop(low, high, body, 0, unroll=8)

    def turn_marks():
        for i in range(TILES // GROUP):
            block = marks[i * GROUP:(i + 1) * GROUP].reshape(GROUP * 8, 128)
            select[i] = block.T[:SLOTS].astype(bf16)

    def spread_pert():
        for copy in near_copies:
            copy.wait()

        def body(s, carry):
            pert_f[s] = pert_raw[s].astype(f32)
            return carry

        lax.fori_loop(0, SLOTS, body, 0, unroll=2)

    def arrange(u):
        k = UNITS[u][0]
        for part in range(len(PARTS)):
            for item in held[u, part]:
                settle(item[3])
        order = [
            {"y": dy, "x": dx, "z": dz}
            for dy in distances(UNITS[u], "y")
            for dx in distances(UNITS[u], "x")
            for dz in distances(UNITS[u], "z")
        ]
        for i, by in enumerate(order):
            source = place({n: (here[n] - by[n] + SIZE[n]) % SIZE[n] for n in NAMES})
            pert_u[:, pl.ds(i, 1), :] = pert_f[:, pl.ds(source * 2 + k, 1), :]
        for part, (low, high) in enumerate(PARTS):
            refs = []
            for by in order:
                found = [item for item in held[u, part] if item[0] == by]
                ref = found[0][1]
                if not any(by.values()):
                    ref = own.at[k, pl.ds(low, high - low)]
                refs.append(ref)

            def body(j, carry, low=low, refs=refs):
                pair = low + j
                g = grad[pair]
                for i in range(0, len(refs), 2):
                    one = refs[i][j].astype(f32) * g
                    two = refs[i + 1][j].astype(f32) * g
                    scaled[2 * pair, i * 8:i * 8 + 16, :] = jnp.concatenate([one[:8], two[:8]], 0).astype(bf16)
                    scaled[2 * pair + 1, i * 8:i * 8 + 16, :] = jnp.concatenate([one[8:], two[8:]], 0).astype(bf16)
                return carry

            lax.fori_loop(0, high - low, body, 0)

    def scores(first):
        results = []
        left = [scaled[block_ref[first + i]] for i in range(GROUP)]
        right = [tiles[first + i] for i in range(GROUP)]
        products = [jnp.dot(left[i], right[i], preferred_element_type=f32) for i in range(GROUP)]
        for i in range(GROUP):
            weight = pert_u[owner_ref[first + i] % SLOTS]
            results.append(jnp.sum(products[i].reshape(8, 8, 128) * weight[:, None, :], axis=0))
        return results

    def work(u, low, high):
        def body(i, carry):
            first = i * GROUP
            results = scores(first)
            if u > 0:
                before = [total[first + j] for j in range(GROUP)]
                results = [results[j] + before[j] for j in range(GROUP)]
            for j in range(GROUP):
                total[first + j] = results[j]
            return carry

        lax.fori_loop(low, high, body, 0)

    def work_last():
        def body(i, carry):
            first = i * GROUP
            results = scores(first)
            results = [(results[j] + total[first + j]) * vert_f[first + j] for j in range(GROUP)]
            value = jnp.concatenate(results, axis=0)
            high = value.astype(bf16)
            low = (value - high.astype(f32)).astype(bf16)
            chosen = select[i]
            carry = carry + jnp.dot(chosen, high, preferred_element_type=f32)
            return carry + jnp.dot(chosen, low, preferred_element_type=f32)

        return lax.fori_loop(0, TILES // GROUP, body, jnp.zeros((SLOTS, 128), f32))

    jobs = [ready_local]
    jobs += [functools.partial(turn_tiles, i, i + 32) for i in range(0, TILES, 32)]
    jobs += [spread_vert]
    jobs += [functools.partial(mark_owners, i, i + 128) for i in range(0, TILES, 128)]
    jobs += [turn_marks, spread_pert]

    def next_job():
        if jobs:
            jobs.pop(0)()

    last = len(UNITS) - 1
    pending = 0
    for tick in range(last + 1 + 3 * LAG):
        if tick <= last:
            begin(tick)
        done = tick - 3 * LAG
        if done == 0:
            while jobs:
                next_job()
        if 0 <= done < last:
            jobs.append(functools.partial(arrange, done))
            pieces = TILES // GROUP // 4
            jobs += [functools.partial(work, done, i * pieces, (i + 1) * pieces) for i in range(4)]
        for part in range(len(PARTS)):
            for stage in (2, 1, 0):
                u = tick - stage * LAG
                if 0 <= u <= last:
                    advance(u, part, stage, tick)
                    if tick > 0:
                        next_job()
        if tick == 0:
            for copy in near_copies:
                copy.start()
        if done >= 0:
            while jobs:
                next_job()
        while pending < len(sent) and sent[pending][0] <= tick - 2:
            sent[pending][1].wait_send()
            pending += 1
    while pending < len(sent):
        sent[pending][1].wait_send()
        pending += 1
    arrange(last)
    sums = work_last()
    for s in range(SLOTS):
        rows[s] = sums[s:s + 1]
    back = []
    for i, to in enumerate(near):
        back.append(
            pltpu.make_async_remote_copy(
                src_ref=rows.at[(to[0] * N_LEV + to[1]) % SLOTS],
                dst_ref=arrived.at[i],
                send_sem=back_send.at[i],
                recv_sem=back_recv.at[i],
                device_id=to,
                device_id_type=MESH,
            )
        )
    for copy in back:
        copy.start()
    for copy in back:
        copy.wait_recv()
    whole = rows[my_slot]
    for i in range(len(NEAR)):
        whole = whole + arrived[i]
    out_ref[...] = whole
    for copy in back:
        copy.wait_send()


def local(
    members,
    gradient,
    horiz_loc,
    vert_loc,
    tile_block,
    tile_obs,
    tile_live,
    obs_pert,
    innovation,
    obs_error,
    obs_count,
):
    f32, bf16 = jnp.float32, jnp.bfloat16
    side = 128
    held, levels, columns = members.shape
    moving = members.reshape(held, levels, columns // side, side).transpose(0, 2, 1, 3)
    moving = moving.reshape(held, 2, 2, 2, 2, 2, 32, 16, side)
    slopes = gradient.reshape(levels, 64, side).transpose(1, 0, 2).reshape(32, 16, side)
    vertical = vert_loc.reshape(TILES // 2, 16, side)
    units, parts, count, close = len(UNITS), len(PARTS), moves(), len(NEAR)
    anywhere = pl.BlockSpec(memory_space=pl.ANY)
    scalar = pl.BlockSpec(memory_space=pltpu.SMEM)
    dma = pltpu.SemaphoreType.DMA
    raw_sum = pl.pallas_call(
        kernel,
        name="efsoi",
        out_shape=jax.ShapeDtypeStruct((1, side), f32),
        in_specs=[anywhere] * 4 + [scalar] * 3 + [anywhere],
        out_specs=pl.BlockSpec(memory_space=pltpu.VMEM),
        scratch_shapes=[
            pltpu.VMEM((units, parts, 2, 2, 2, WIDEST, 16, side), bf16),
            pltpu.VMEM((units, parts, 4, 2, WIDEST, 16, side), bf16),
            pltpu.VMEM((units, parts, 8, WIDEST, 16, side), bf16),
            pltpu.VMEM((2, 32, 16, side), bf16),
            pltpu.VMEM((32, 16, side), f32),
            pltpu.VMEM((TILES, side, side), bf16),
            pltpu.VMEM((TILES // 2, 16, side), bf16),
            pltpu.VMEM((TILES, 8, side), f32),
            pltpu.VMEM((64, 64, side), bf16),
            pltpu.VMEM((TILES, 8, side), f32),
            pltpu.VMEM((SLOTS, 64, side), bf16),
            pltpu.VMEM((SLOTS, 64, side), f32),
            pltpu.VMEM((SLOTS, 8, side), f32),
            pltpu.VMEM((TILES, 8, side), f32),
            pltpu.VMEM((TILES // GROUP, SLOTS, side), bf16),
            pltpu.VMEM((SLOTS, 1, side), f32),
            pltpu.VMEM((close, 1, side), f32),
            dma((count,)),
            dma((count,)),
            dma((close,)),
            dma((close,)),
            dma((close,)),
            dma((close,)),
            dma((5,)),
        ],
        compiler_params=pltpu.CompilerParams(
            collective_id=0, has_side_effects=True, vmem_limit_bytes=56 << 20
        ),
        cost_estimate=pl.CostEstimate(
            flops=2 * TILES * 512 * side * side, bytes_accessed=32 << 20, transcendentals=0
        ),
    )(moving, slopes, horiz_loc, vertical, tile_block, tile_obs, tile_live, obs_pert)
    sensitivity = raw_sum.reshape(side) / (64 - 1)
    observed = jnp.arange(side, dtype=jnp.int32) < obs_count[0]
    sensitivity = jnp.where(observed, sensitivity, jnp.zeros_like(sensitivity))
    impact = innovation * sensitivity / obs_error
    return (sensitivity, impact)


def solution(mesh):
    both = ("pts", "lev")
    placed = (
        P("pts", "lev", None),
        P("lev", "pts"),
        P(both, None, None),
        P(both, None, None),
        P(both),
        P(both),
        P(both),
        P(None, both),
        P(both),
        P(both),
        P(both),
    )
    return jax.shard_map(
        local,
        mesh=mesh,
        in_specs=placed,
        out_specs=(P(both), P(both)),
        check_vma=False,
    )
```

```python
import functools

import jax
import jax.numpy as jnp
from jax import lax
from jax.experimental import pallas as pl
from jax.experimental.pallas import tpu as pltpu
from jax.sharding import PartitionSpec as P

MESH = pl.DeviceIdType.MESH
REACH = 2
N_PTS = 32
N_LEV = 4
SIZE = {"y": 2, "x": 4, "z": 4}
NAMES = ("y", "x", "z")
PARTS = ((0, 11), (11, 22), (22, 32))
WIDEST = 11
ORDERS = (("x", "z", "y"), ("z", "y", "x"), ("y", "x", "z"))
UNITS = tuple((k, a, b) for k in (0, 1) for a in (0, 1) for b in (0, 1))
LAG = 2
TILES = 256
GROUP = 32
LAST_GROUP = 64
SLOTS = 32


def distances(unit, axis):
    k, a, b = unit
    return {"y": (0, 1), "x": (a, a + 2), "z": (b, b + 2)}[axis]


def moves():
    count = 0
    for u, unit in enumerate(UNITS):
        for part in range(len(PARTS)):
            held = 1
            for axis in ORDERS[(part + u) % 3]:
                count += held * sum(1 for step in distances(unit, axis) if step)
                held *= 2
    return count


NEAR = [(o, r) for o in range(-REACH, REACH + 1) for r in range(N_LEV) if (o, r) != (0, 0)]


def kernel(
    members, gradient, horiz, vert, block_ref, owner_ref, live_ref, pert,
    out_ref,
    hop1, hop2, hop3, own, grad, tiles, vert_raw, vert_f, scaled, total,
    pert_raw, pert_f, pert_u, marks, select, rows, arrived,
    send_sem, recv_sem, pert_send, pert_recv, back_send, back_recv, local_sem,
):
    f32, bf16 = jnp.float32, jnp.bfloat16
    me, lev = lax.axis_index("pts"), lax.axis_index("lev")
    here = {"y": me // 16, "x": (me // 4) % 4, "z": me % 4}
    my_slot = (me * N_LEV + lev) % SLOTS
    chip, core = lev // 2, lev % 2

    def place(at):
        return at["y"] * 16 + at["x"] * 4 + at["z"]

    def moved(axis, step):
        at = dict(here)
        at[axis] = (at[axis] + step) % SIZE[axis]
        return place(at)

    local_copies = [
        pltpu.make_async_copy(horiz, tiles, local_sem.at[0]),
        pltpu.make_async_copy(gradient, grad, local_sem.at[1]),
        pltpu.make_async_copy(vert, vert_raw, local_sem.at[2]),
        pltpu.make_async_copy(pert, pert_raw.at[chip, core, REACH], local_sem.at[3]),
        pltpu.make_async_copy(
            members.at[:, here["y"], here["x"] // 2, here["x"] % 2, here["z"] // 2, here["z"] % 2],
            own,
            local_sem.at[4],
        ),
    ]

    barrier = pltpu.get_barrier_semaphore()
    line = [("x", 1), ("x", 2), ("x", 3), ("z", 1), ("z", 2), ("z", 3), ("y", 1)]
    for axis, step in line:
        pl.semaphore_signal(barrier, inc=1, device_id={"pts": moved(axis, step)}, device_id_type=MESH)
    near = [((me + o + N_PTS) % N_PTS, (lev + r) % N_LEV) for o, r in NEAR]
    for to in near:
        pl.semaphore_signal(barrier, inc=1, device_id=to, device_id_type=MESH)
    for copy in local_copies:
        copy.start()
    pl.semaphore_wait(barrier, len(line) + len(near))

    def pert_copy(i, source, there, to):
        return pltpu.make_async_remote_copy(
            src_ref=source,
            dst_ref=there,
            send_sem=pert_send.at[i],
            recv_sem=pert_recv.at[i],
            device_id=to,
            device_id_type=MESH,
        )

    pert_along = [
        pert_copy(i, pert, pert_raw.at[chip, core, REACH - o], {"pts": (me + o + N_PTS) % N_PTS})
        for i, o in enumerate((1, -1, 2, -2))
    ]
    pert_across = pert_copy(4, pert_raw.at[chip, core], pert_raw.at[chip, core], {"lev": (lev + 2) % N_LEV})
    pert_beside = pert_copy(5, pert_raw.at[:, core], pert_raw.at[:, core], {"lev": lev + 1 - 2 * core})

    hops = (hop1, hop2, hop3)
    held = {}
    sent = []

    def begin(u):
        k, a, b = UNITS[u]
        for part, (low, high) in enumerate(PARTS):
            base = members.at[
                k, :, :, (here["x"] + a) % 2, :, (here["z"] + b) % 2, pl.ds(low, high - low)
            ]
            held[u, part] = [({}, base, NAMES, None)]

    def settle(entry):
        if entry is not None and not entry[1]:
            entry[0].wait_recv()
            entry[1] = True

    def advance(u, part, stage, tick):
        low, high = PARTS[part]
        axis = ORDERS[(part + u) % 3][stage]
        fresh, slot = [], 0
        for moved_by, ref, left, entry in held[u, part]:
            settle(entry)
            for step in distances(UNITS[u], axis):
                target = (here[axis] + step) % SIZE[axis]
                index = target if axis == "y" else target // 2
                source = ref.at[tuple(index if n == axis else slice(None) for n in left)]
                rest = tuple(n for n in left if n != axis)
                by = {**moved_by, axis: step}
                if step == 0:
                    fresh.append((by, source, rest, entry))
                    continue
                there = hops[stage].at[
                    (u, part, slot) + (slice(None),) * len(rest) + (pl.ds(0, high - low),)
                ]
                copy = pltpu.make_async_remote_copy(
                    src_ref=source,
                    dst_ref=there,
                    send_sem=send_sem.at[len(sent)],
                    recv_sem=recv_sem.at[len(sent)],
                    device_id={"pts": moved(axis, step)},
                    device_id_type=MESH,
                )
                copy.start()
                sent.append((tick, copy))
                fresh.append((by, there, rest, [copy, False]))
                slot += 1
        held[u, part] = fresh


    def ready_local():
        for copy in local_copies:
            copy.wait()

    def turn_tiles(low, high):
        def body(i, carry):
            turned = [tiles[i * 4 + j].T for j in range(4)]
            for j in range(4):
                tiles[i * 4 + j] = turned[j]
            return carry

        lax.fori_loop(low // 4, high // 4, body, 0)

    def spread_vert():
        def body(i, carry):
            both = vert_raw[i].astype(f32)
            vert_f[2 * i] = both[:8]
            vert_f[2 * i + 1] = both[8:]
            return carry

        lax.fori_loop(0, TILES // 2, body, 0, unroll=4)

    def mark_owners(low, high):
        lanes = lax.broadcasted_iota(jnp.int32, (8, 128), 1)
        live = live_ref[0]

        def body(t, carry):
            slot = owner_ref[t] % SLOTS
            slot = jnp.where(t < live, slot, -1)
            marks[t] = jnp.where(lanes == slot, 1.0, 0.0).astype(f32)
            return carry

        lax.fori_loop(low, high, body, 0, unroll=8)

    def turn_marks():
        for i in range(TILES // 16):
            block = marks[i * 16:(i + 1) * 16].reshape(128, 128)
            group, at = divmod(i, LAST_GROUP // 16)
            select[group, :, at * 128:(at + 1) * 128] = block.T[:SLOTS].astype(bf16)

    def pert_second():
        for copy in pert_along:
            copy.wait_recv()
        pert_across.start()

    def pert_third():
        pert_across.wait_recv()
        pert_beside.start()

    def spread_pert():
        pert_beside.wait_recv()
        for copy in pert_along + [pert_across, pert_beside]:
            copy.wait_send()
        for o in range(-REACH, REACH + 1):
            for r in range(N_LEV):
                slot = (me + o + N_PTS) % (SLOTS // N_LEV) * N_LEV + r
                pert_f[slot] = pert_raw[r // 2, r % 2, o + REACH].astype(f32)

    def sources(u):
        return [
            {"y": dy, "x": dx, "z": dz}
            for dy in distances(UNITS[u], "y")
            for dx in distances(UNITS[u], "x")
            for dz in distances(UNITS[u], "z")
        ]

    def order_pert(u):
        for i, by in enumerate(sources(u)):
            source = place({n: (here[n] - by[n] + SIZE[n]) % SIZE[n] for n in NAMES})
            pert_u[u, :, pl.ds(i, 1), :] = pert_f[:, pl.ds(source * 2 + UNITS[u][0], 1), :]

    def arrange(u):
        for part, (low, high) in enumerate(PARTS):
            refs = []
            for by in sources(u):
                ref, entry = [(item[1], item[3]) for item in held[u, part] if item[0] == by][0]
                settle(entry)
                if not any(by.values()):
                    ref = own.at[UNITS[u][0], pl.ds(low, high - low)]
                refs.append(ref)

            def body(j, carry, low=low, refs=refs):
                pair = low + j
                g = grad[pair]
                for i in range(0, len(refs), 2):
                    one = refs[i][j].astype(f32) * g
                    two = refs[i + 1][j].astype(f32) * g
                    scaled[2 * pair, i * 8:i * 8 + 16, :] = jnp.concatenate([one[:8], two[:8]], 0).astype(bf16)
                    scaled[2 * pair + 1, i * 8:i * 8 + 16, :] = jnp.concatenate([one[8:], two[8:]], 0).astype(bf16)
                return carry

            lax.fori_loop(0, high - low, body, 0)

    def scores(u, first, size):
        results = []
        left = [scaled[block_ref[first + i]] for i in range(size)]
        right = [tiles[first + i] for i in range(size)]
        products = [jnp.dot(left[i], right[i], preferred_element_type=f32) for i in range(size)]
        for i in range(size):
            weight = pert_u[u, owner_ref[first + i] % SLOTS]
            results.append(jnp.sum(products[i].reshape(8, 8, 128) * weight[:, None, :], axis=0))
        return results

    def work(u, low, high):
        def body(i, carry):
            first = i * GROUP
            results = scores(u, first, GROUP)
            if u > 0:
                before = [total[first + j] for j in range(GROUP)]
                results = [results[j] + before[j] for j in range(GROUP)]
            for j in range(GROUP):
                total[first + j] = results[j]
            return carry

        lax.fori_loop(low, high, body, 0)

    def work_last():
        def body(i, carry):
            first = i * LAST_GROUP
            results = scores(last, first, LAST_GROUP)
            results = [(results[j] + total[first + j]) * vert_f[first + j] for j in range(LAST_GROUP)]
            value = jnp.concatenate(results, axis=0)
            high = value.astype(bf16)
            low = (value - high.astype(f32)).astype(bf16)
            chosen = select[i]
            carry = carry + jnp.dot(chosen, high, preferred_element_type=f32)
            return carry + jnp.dot(chosen, low, preferred_element_type=f32)

        return lax.fori_loop(0, TILES // LAST_GROUP, body, jnp.zeros((SLOTS, 128), f32))

    last = len(UNITS) - 1
    turns = [functools.partial(turn_tiles, i, i + 32) for i in range(0, TILES, 32)]
    jobs = [ready_local] + turns[:2] + [pert_second] + turns[2:7] + [pert_third] + turns[7:]
    jobs += [spread_vert]
    jobs += [functools.partial(mark_owners, i, i + 128) for i in range(0, TILES, 128)]
    jobs += [turn_marks, spread_pert]
    jobs += [functools.partial(order_pert, u) for u in range(len(UNITS))]

    def next_job():
        if jobs:
            jobs.pop(0)()

    pending = 0
    for tick in range(last + 1 + 3 * LAG):
        if tick <= last:
            begin(tick)
        done = tick - 3 * LAG
        if done == 0:
            while jobs:
                next_job()
        if 0 <= done < last:
            jobs.append(functools.partial(arrange, done))
            pieces = TILES // GROUP // 4
            jobs += [functools.partial(work, done, i * pieces, (i + 1) * pieces) for i in range(4)]
        for part in range(len(PARTS)):
            for stage in (2, 1, 0):
                u = tick - stage * LAG
                if 0 <= u <= last:
                    advance(u, part, stage, tick)
                    if tick > 0:
                        next_job()
        if tick == 0:
            for copy in pert_along:
                copy.start()
        if done >= 0:
            while jobs:
                next_job()
        while pending < len(sent) and sent[pending][0] <= tick - 2:
            sent[pending][1].wait_send()
            pending += 1
    arrange(last)
    sums = work_last()
    for s in range(SLOTS):
        rows[s] = sums[s:s + 1]
    back = []
    for i, to in enumerate(near):
        back.append(
            pltpu.make_async_remote_copy(
                src_ref=rows.at[(to[0] * N_LEV + to[1]) % SLOTS],
                dst_ref=arrived.at[i],
                send_sem=back_send.at[i],
                recv_sem=back_recv.at[i],
                device_id=to,
                device_id_type=MESH,
            )
        )
    for copy in back:
        copy.start()
    for copy in back:
        copy.wait_recv()
    whole = rows[my_slot]
    for i in range(len(NEAR)):
        whole = whole + arrived[i]
    out_ref[...] = whole
    for copy in back:
        copy.wait_send()
    for tick, copy in sent[pending:]:
        copy.wait_send()


def local(
    members,
    gradient,
    horiz_loc,
    vert_loc,
    tile_block,
    tile_obs,
    tile_live,
    obs_pert,
    innovation,
    obs_error,
    obs_count,
):
    f32, bf16 = jnp.float32, jnp.bfloat16
    side = 128
    held, levels, columns = members.shape
    moving = members.reshape(held, levels, columns // side, side).transpose(0, 2, 1, 3)
    moving = moving.reshape(held, 2, 2, 2, 2, 2, 32, 16, side)
    slopes = gradient.reshape(levels, 64, side).transpose(1, 0, 2).reshape(32, 16, side)
    vertical = vert_loc.reshape(TILES // 2, 16, side)
    units, parts, count, close = len(UNITS), len(PARTS), moves(), len(NEAR)
    anywhere = pl.BlockSpec(memory_space=pl.ANY)
    scalar = pl.BlockSpec(memory_space=pltpu.SMEM)
    dma = pltpu.SemaphoreType.DMA
    raw_sum = pl.pallas_call(
        kernel,
        name="efsoi",
        out_shape=jax.ShapeDtypeStruct((1, side), f32),
        in_specs=[anywhere] * 4 + [scalar] * 3 + [anywhere],
        out_specs=pl.BlockSpec(memory_space=pltpu.VMEM),
        scratch_shapes=[
            pltpu.VMEM((units, parts, 2, 2, 2, WIDEST, 16, side), bf16),
            pltpu.VMEM((units, parts, 4, 2, WIDEST, 16, side), bf16),
            pltpu.VMEM((units, parts, 8, WIDEST, 16, side), bf16),
            pltpu.VMEM((2, 32, 16, side), bf16),
            pltpu.VMEM((32, 16, side), f32),
            pltpu.VMEM((TILES, side, side), bf16),
            pltpu.VMEM((TILES // 2, 16, side), bf16),
            pltpu.VMEM((TILES, 8, side), f32),
            pltpu.VMEM((64, 64, side), bf16),
            pltpu.VMEM((TILES, 8, side), f32),
            pltpu.VMEM((2, 2, 2 * REACH + 1, 64, side), bf16),
            pltpu.VMEM((SLOTS, 64, side), f32),
            pltpu.VMEM((units, SLOTS, 8, side), f32),
            pltpu.VMEM((TILES, 8, side), f32),
            pltpu.VMEM((TILES // LAST_GROUP, SLOTS, LAST_GROUP * 8), bf16),
            pltpu.VMEM((SLOTS, 1, side), f32),
            pltpu.VMEM((close, 1, side), f32),
            dma((count,)),
            dma((count,)),
            dma((6,)),
            dma((6,)),
            dma((close,)),
            dma((close,)),
            dma((5,)),
        ],
        compiler_params=pltpu.CompilerParams(
            collective_id=0, has_side_effects=True, vmem_limit_bytes=56 << 20
        ),
        cost_estimate=pl.CostEstimate(
            flops=2 * TILES * 512 * side * side, bytes_accessed=32 << 20, transcendentals=0
        ),
    )(moving, slopes, horiz_loc, vertical, tile_block, tile_obs, tile_live, obs_pert)
    sensitivity = raw_sum.reshape(side) / (64 - 1)
    observed = jnp.arange(side, dtype=jnp.int32) < obs_count[0]
    sensitivity = jnp.where(observed, sensitivity, jnp.zeros_like(sensitivity))
    impact = innovation * sensitivity / obs_error
    return (sensitivity, impact)


def solution(mesh):
    both = ("pts", "lev")
    placed = (
        P("pts", "lev", None),
        P("lev", "pts"),
        P(both, None, None),
        P(both, None, None),
        P(both),
        P(both),
        P(both),
        P(None, both),
        P(both),
        P(both),
        P(both),
    )
    return jax.shard_map(
        local,
        mesh=mesh,
        in_specs=placed,
        out_specs=(P(both), P(both)),
        check_vma=False,
    )
```

```python
import functools

import jax
import jax.numpy as jnp
from jax import lax
from jax.experimental import pallas as pl
from jax.experimental.pallas import tpu as pltpu
from jax.sharding import PartitionSpec as P

MESH = pl.DeviceIdType.MESH
REACH = 2
N_PTS = 32
N_LEV = 4
SIZE = {"y": 2, "x": 4, "z": 4}
NAMES = ("y", "x", "z")
PARTS = ((0, 11), (11, 22), (22, 32))
WIDEST = 11
ORDERS = (("x", "y", "z"), ("y", "z", "x"), ("z", "x", "y"))
UNITS = tuple((k, a, b) for k in (0, 1) for a in (0, 1) for b in (0, 1))
LAG = 2
PASSES = ((0, 1), (2, 3), (4, 5), (6,), (7,))
WIDTH = max(len(units) for units in PASSES)
TILES = 256
FLUSH = 12
GROUP = 32
LAST_GROUP = 128
SLOTS = 32


def distances(unit, axis):
    k, a, b = unit
    return {"y": (0, 1), "x": (a, a + 2), "z": (b, b + 2)}[axis]


def moves():
    count = 0
    for u, unit in enumerate(UNITS):
        for part in range(len(PARTS)):
            held = 1
            for axis in ORDERS[(part + u) % 3]:
                count += held * sum(1 for step in distances(unit, axis) if step)
                held *= 2
    return count


NEAR = [(o, r) for o in (2, -2, 1, -1, 0) for r in (2, 3, 1, 0) if (o, r) != (0, 0)]


def kernel(
    members, gradient, horiz, vert, block_ref, owner_ref, live_ref, pert,
    out_ref,
    hop1, hop2, hop3, own, grad, tiles, vert_raw, vert_f, scaled, total,
    pert_raw, pert_f, pert_u, marks, select, rows, arrived,
    send_sem, recv_sem, pert_send, pert_recv, back_send, back_recv, local_sem,
):
    f32, bf16 = jnp.float32, jnp.bfloat16
    me, lev = lax.axis_index("pts"), lax.axis_index("lev")
    here = {"y": me // 16, "x": (me // 4) % 4, "z": me % 4}
    my_slot = (me * N_LEV + lev) % SLOTS
    chip, core = lev // 2, lev % 2

    def place(at):
        return at["y"] * 16 + at["x"] * 4 + at["z"]

    def moved(axis, step):
        at = dict(here)
        at[axis] = (at[axis] + step) % SIZE[axis]
        return place(at)

    local_copies = [
        pltpu.make_async_copy(horiz, tiles, local_sem.at[0]),
        pltpu.make_async_copy(gradient, grad, local_sem.at[1]),
        pltpu.make_async_copy(vert, vert_raw, local_sem.at[2]),
        pltpu.make_async_copy(pert, pert_raw.at[chip, core, REACH], local_sem.at[3]),
        pltpu.make_async_copy(
            members.at[:, here["y"], here["x"] // 2, here["x"] % 2, here["z"] // 2, here["z"] % 2],
            own,
            local_sem.at[4],
        ),
    ]

    barrier = pltpu.get_barrier_semaphore()
    line = [("x", 1), ("x", 2), ("x", 3), ("z", 1), ("z", 2), ("z", 3), ("y", 1)]
    for axis, step in line:
        pl.semaphore_signal(barrier, inc=1, device_id={"pts": moved(axis, step)}, device_id_type=MESH)
    near = [((me + o + N_PTS) % N_PTS, (lev + r) % N_LEV) for o, r in NEAR]
    for to in near:
        pl.semaphore_signal(barrier, inc=1, device_id=to, device_id_type=MESH)
    for copy in local_copies:
        copy.start()
    pl.semaphore_wait(barrier, len(line) + len(near))

    def pert_copy(i, source, there, to):
        return pltpu.make_async_remote_copy(
            src_ref=source,
            dst_ref=there,
            send_sem=pert_send.at[i],
            recv_sem=pert_recv.at[i],
            device_id=to,
            device_id_type=MESH,
        )

    pert_along = [
        pert_copy(i, pert, pert_raw.at[chip, core, REACH - o], {"pts": (me + o + N_PTS) % N_PTS})
        for i, o in enumerate((1, -1, 2, -2))
    ]
    pert_across = pert_copy(4, pert_raw.at[chip, core], pert_raw.at[chip, core], {"lev": (lev + 2) % N_LEV})
    pert_beside = pert_copy(5, pert_raw.at[:, core], pert_raw.at[:, core], {"lev": lev + 1 - 2 * core})

    hops = (hop1, hop2, hop3)
    held = {}
    sent = []

    def begin(u):
        k, a, b = UNITS[u]
        for part, (low, high) in enumerate(PARTS):
            base = members.at[
                k, :, :, (here["x"] + a) % 2, :, (here["z"] + b) % 2, pl.ds(low, high - low)
            ]
            held[u, part] = [({}, base, NAMES, None)]

    def settle(entry):
        if entry is not None and not entry[1]:
            entry[0].wait_recv()
            entry[1] = True

    def advance(u, part, stage, tick):
        low, high = PARTS[part]
        axis = ORDERS[(part + u) % 3][stage]
        fresh, slot = [], 0
        for moved_by, ref, left, entry in held[u, part]:
            settle(entry)
            for step in distances(UNITS[u], axis):
                target = (here[axis] + step) % SIZE[axis]
                index = target if axis == "y" else target // 2
                source = ref.at[tuple(index if n == axis else slice(None) for n in left)]
                rest = tuple(n for n in left if n != axis)
                by = {**moved_by, axis: step}
                if step == 0:
                    fresh.append((by, source, rest, entry))
                    continue
                assert slot < (2, 4, 8)[stage]
                there = hops[stage].at[
                    (u, part, slot) + (slice(None),) * len(rest) + (pl.ds(0, high - low),)
                ]
                copy = pltpu.make_async_remote_copy(
                    src_ref=source,
                    dst_ref=there,
                    send_sem=send_sem.at[len(sent)],
                    recv_sem=recv_sem.at[len(sent)],
                    device_id={"pts": moved(axis, step)},
                    device_id_type=MESH,
                )
                copy.start()
                sent.append((tick, copy))
                fresh.append((by, there, rest, [copy, False]))
                slot += 1
        held[u, part] = fresh


    def ready_local():
        for copy in local_copies:
            copy.wait()

    def turn_tiles(low, high):
        def body(i, carry):
            turned = [tiles[i * 4 + j].T for j in range(4)]
            for j in range(4):
                tiles[i * 4 + j] = turned[j]
            return carry

        lax.fori_loop(low // 4, high // 4, body, 0)

    def spread_vert():
        def body(i, carry):
            both = vert_raw[i].astype(f32)
            vert_f[2 * i] = both[:8]
            vert_f[2 * i + 1] = both[8:]
            return carry

        lax.fori_loop(0, TILES // 2, body, 0, unroll=4)

    def mark_owners(low, high):
        lanes = lax.broadcasted_iota(jnp.int32, (8, 128), 1)
        live = live_ref[0]

        def body(t, carry):
            slot = owner_ref[t] % SLOTS
            slot = jnp.where(t < live, slot, -1)
            marks[t] = jnp.where(lanes == slot, 1.0, 0.0).astype(f32)
            return carry

        lax.fori_loop(low, high, body, 0, unroll=8)

    def turn_marks():
        for i in range(TILES // 16):
            block = marks[i * 16:(i + 1) * 16].reshape(128, 128)
            group, at = divmod(i, LAST_GROUP // 16)
            select[group, :, at * 128:(at + 1) * 128] = block.T[:SLOTS].astype(bf16)

    def pert_second():
        for copy in pert_along:
            copy.wait_recv()
        pert_across.start()

    def pert_third():
        pert_across.wait_recv()
        pert_beside.start()

    def spread_pert():
        pert_beside.wait_recv()
        for copy in pert_along + [pert_across, pert_beside]:
            copy.wait_send()
        for o in range(-REACH, REACH + 1):
            for r in range(N_LEV):
                slot = (me + o + N_PTS) % (SLOTS // N_LEV) * N_LEV + r
                pert_f[slot] = pert_raw[r // 2, r % 2, o + REACH].astype(f32)

    def sources(u):
        return [
            {"y": dy, "x": dx, "z": dz}
            for dy in distances(UNITS[u], "y")
            for dx in distances(UNITS[u], "x")
            for dz in distances(UNITS[u], "z")
        ]

    def order_pert(u):
        for i, by in enumerate(sources(u)):
            source = place({n: (here[n] - by[n] + SIZE[n]) % SIZE[n] for n in NAMES})
            p, at = places[u]
            pert_u[p, :, pl.ds(at * 8 + i, 1), :] = pert_f[:, pl.ds(source * 2 + UNITS[u][0], 1), :]

    places = {u: (p, at) for p, units in enumerate(PASSES) for at, u in enumerate(units)}

    def arrange(u):
        row = places[u][1] * 64
        for part, (low, high) in enumerate(PARTS):
            refs = []
            for by in sources(u):
                ref, entry = [(item[1], item[3]) for item in held[u, part] if item[0] == by][0]
                settle(entry)
                if not any(by.values()):
                    ref = own.at[UNITS[u][0], pl.ds(low, high - low)]
                refs.append(ref)

            def body(j, carry, low=low, refs=refs, row=row):
                pair = low + j
                g = grad[pair]
                for i in range(0, len(refs), 2):
                    one = refs[i][j].astype(f32) * g
                    two = refs[i + 1][j].astype(f32) * g
                    scaled[2 * pair, row + i * 8:row + i * 8 + 16, :] = jnp.concatenate([one[:8], two[:8]], 0).astype(bf16)
                    scaled[2 * pair + 1, row + i * 8:row + i * 8 + 16, :] = jnp.concatenate([one[8:], two[8:]], 0).astype(bf16)
                return carry

            lax.fori_loop(0, high - low, body, 0)

    def scores(p, first, size):
        results = []
        held_members = 8 * len(PASSES[p])
        left = [scaled[block_ref[first + i], :8 * held_members] for i in range(size)]
        right = [tiles[first + i] for i in range(size)]
        products = [jnp.dot(left[i], right[i], preferred_element_type=f32) for i in range(size)]
        for i in range(size):
            weight = pert_u[p, owner_ref[first + i] % SLOTS, :held_members]
            results.append(jnp.sum(products[i].reshape(held_members, 8, 128) * weight[:, None, :], axis=0))
        return results

    def work(p, low, high):
        def body(i, carry):
            first = i * GROUP
            results = scores(p, first, GROUP)
            if p > 0:
                before = [total[first + j] for j in range(GROUP)]
                results = [results[j] + before[j] for j in range(GROUP)]
            for j in range(GROUP):
                total[first + j] = results[j]
            return carry

        lax.fori_loop(low, high, body, 0)

    def work_last():
        def body(i, carry):
            first = i * LAST_GROUP
            results = scores(len(PASSES) - 1, first, LAST_GROUP)
            results = [(results[j] + total[first + j]) * vert_f[first + j] for j in range(LAST_GROUP)]
            value = jnp.concatenate(results, axis=0)
            high = value.astype(bf16)
            low = (value - high.astype(f32)).astype(bf16)
            chosen = select[i]
            carry = carry + jnp.dot(chosen, high, preferred_element_type=f32)
            return carry + jnp.dot(chosen, low, preferred_element_type=f32)

        return lax.fori_loop(0, TILES // LAST_GROUP, body, jnp.zeros((SLOTS, 128), f32))

    last = len(UNITS) - 1
    turns = [functools.partial(turn_tiles, i, i + 32) for i in range(0, TILES, 32)]
    jobs = [ready_local] + turns[:2] + [pert_second] + turns[2:7] + [pert_third] + turns[7:]
    jobs += [spread_vert]
    jobs += [functools.partial(mark_owners, i, i + 128) for i in range(0, TILES, 128)]
    jobs += [turn_marks, spread_pert]
    jobs += [functools.partial(order_pert, u) for u in range(len(UNITS))]

    def next_job():
        if jobs:
            jobs.pop(0)()

    pending = 0
    for tick in range(last + 1 + 3 * LAG):
        if tick <= last:
            begin(tick)
        done = tick - 3 * LAG
        if done == 0:
            while jobs:
                next_job()
        if 0 <= done < last:
            jobs.append(functools.partial(arrange, done))
            p, at = places[done]
            if at == len(PASSES[p]) - 1:
                jobs += [functools.partial(work, p, i, i + 1) for i in range(TILES // GROUP)]
        for part in range(len(PARTS)):
            for stage in (2, 1, 0):
                u = tick - stage * LAG
                if 0 <= u <= last:
                    advance(u, part, stage, tick)
                    if tick > 0:
                        next_job()
        if tick == 0:
            for copy in pert_along:
                copy.start()
        if tick >= FLUSH:
            while jobs:
                next_job()
        while pending < len(sent) and sent[pending][0] <= tick - 2:
            sent[pending][1].wait_send()
            pending += 1
    arrange(last)
    sums = work_last()
    for s in range(SLOTS):
        rows[s] = sums[s:s + 1]
    back = []
    for i, to in enumerate(near):
        back.append(
            pltpu.make_async_remote_copy(
                src_ref=rows.at[(to[0] * N_LEV + to[1]) % SLOTS],
                dst_ref=arrived.at[i],
                send_sem=back_send.at[i],
                recv_sem=back_recv.at[i],
                device_id=to,
                device_id_type=MESH,
            )
        )
    for copy in back:
        copy.start()
    for copy in back:
        copy.wait_recv()
    whole = rows[my_slot]
    for i in range(len(NEAR)):
        whole = whole + arrived[i]
    out_ref[...] = whole
    for copy in back:
        copy.wait_send()
    for tick, copy in sent[pending:]:
        copy.wait_send()


def local(
    members,
    gradient,
    horiz_loc,
    vert_loc,
    tile_block,
    tile_obs,
    tile_live,
    obs_pert,
    innovation,
    obs_error,
    obs_count,
):
    f32, bf16 = jnp.float32, jnp.bfloat16
    side = 128
    held, levels, columns = members.shape
    moving = members.reshape(held, levels, columns // side, side).transpose(0, 2, 1, 3)
    moving = moving.reshape(held, 2, 2, 2, 2, 2, 32, 16, side)
    slopes = gradient.reshape(levels, 64, side).transpose(1, 0, 2).reshape(32, 16, side)
    vertical = vert_loc.reshape(TILES // 2, 16, side)
    units, parts, count, close = len(UNITS), len(PARTS), moves(), len(NEAR)
    anywhere = pl.BlockSpec(memory_space=pl.ANY)
    scalar = pl.BlockSpec(memory_space=pltpu.SMEM)
    dma = pltpu.SemaphoreType.DMA
    raw_sum = pl.pallas_call(
        kernel,
        name="efsoi",
        out_shape=jax.ShapeDtypeStruct((1, side), f32),
        in_specs=[anywhere] * 4 + [scalar] * 3 + [anywhere],
        out_specs=pl.BlockSpec(memory_space=pltpu.VMEM),
        scratch_shapes=[
            pltpu.VMEM((units, parts, 2, 2, 2, WIDEST, 16, side), bf16),
            pltpu.VMEM((units, parts, 4, 2, WIDEST, 16, side), bf16),
            pltpu.VMEM((units, parts, 8, WIDEST, 16, side), bf16),
            pltpu.VMEM((2, 32, 16, side), bf16),
            pltpu.VMEM((32, 16, side), f32),
            pltpu.VMEM((TILES, side, side), bf16),
            pltpu.VMEM((TILES // 2, 16, side), bf16),
            pltpu.VMEM((TILES, 8, side), f32),
            pltpu.VMEM((64, WIDTH * 64, side), bf16),
            pltpu.VMEM((TILES, 8, side), f32),
            pltpu.VMEM((2, 2, 2 * REACH + 1, 64, side), bf16),
            pltpu.VMEM((SLOTS, 64, side), f32),
            pltpu.VMEM((len(PASSES), SLOTS, WIDTH * 8, side), f32),
            pltpu.VMEM((TILES, 8, side), f32),
            pltpu.VMEM((TILES // LAST_GROUP, SLOTS, LAST_GROUP * 8), bf16),
            pltpu.VMEM((SLOTS, 1, side), f32),
            pltpu.VMEM((close, 1, side), f32),
            dma((count,)),
            dma((count,)),
            dma((6,)),
            dma((6,)),
            dma((close,)),
            dma((close,)),
            dma((5,)),
        ],
        compiler_params=pltpu.CompilerParams(
            collective_id=0, has_side_effects=True, vmem_limit_bytes=56 << 20
        ),
        cost_estimate=pl.CostEstimate(
            flops=2 * TILES * 512 * side * side, bytes_accessed=32 << 20, transcendentals=0
        ),
    )(moving, slopes, horiz_loc, vertical, tile_block, tile_obs, tile_live, obs_pert)
    sensitivity = raw_sum.reshape(side) / (64 - 1)
    observed = jnp.arange(side, dtype=jnp.int32) < obs_count[0]
    sensitivity = jnp.where(observed, sensitivity, jnp.zeros_like(sensitivity))
    impact = innovation * sensitivity / obs_error
    return (sensitivity, impact)


def solution(mesh):
    both = ("pts", "lev")
    placed = (
        P("pts", "lev", None),
        P("lev", "pts"),
        P(both, None, None),
        P(both, None, None),
        P(both),
        P(both),
        P(both),
        P(None, both),
        P(both),
        P(both),
        P(both),
    )
    return jax.shard_map(
        local,
        mesh=mesh,
        in_specs=placed,
        out_specs=(P(both), P(both)),
        check_vma=False,
    )
```

```python
import functools

import jax
import jax.numpy as jnp
from jax import lax
from jax.experimental import pallas as pl
from jax.experimental.pallas import tpu as pltpu
from jax.sharding import PartitionSpec as P

MESH = pl.DeviceIdType.MESH
REACH = 2
N_PTS = 32
N_LEV = 4
SIZE = {"y": 2, "x": 4, "z": 4}
NAMES = ("y", "x", "z")
PARTS = ((0, 11), (11, 22), (22, 32))
WIDEST = 11
ORDERS = (("x", "y", "z"), ("y", "z", "x"), ("z", "x", "y"))
UNITS = tuple((k, a, b) for a in (0, 1) for b in (0, 1) for k in (0, 1))
LAG = 2
PASSES = ((0, 1), (2, 3), (4, 5), (6,), (7,))
WIDTH = max(len(units) for units in PASSES)
TILES = 256
FLUSH = 12
GROUP = 32
LAST_GROUP = 128
SLOTS = 32


def distances(unit, axis):
    k, a, b = unit
    return {"y": (0, 1), "x": (a, a + 2), "z": (b, b + 2)}[axis]


def moves():
    count = 0
    for u, unit in enumerate(UNITS):
        for part in range(len(PARTS)):
            held = 1
            for axis in ORDERS[(part + u) % 3]:
                count += held * sum(1 for step in distances(unit, axis) if step)
                held *= 2
    return count


NEAR = [(o, r) for o in (2, -2, 1, -1, 0) for r in (2, 3, 1, 0) if (o, r) != (0, 0)]


def kernel(
    members, gradient, horiz, vert, block_ref, owner_ref, live_ref, pert,
    out_ref,
    hop1, hop2, hop3, own, grad, tiles, vert_raw, vert_f, scaled, total,
    pert_raw, pert_f, pert_u, marks, select, rows, arrived,
    send_sem, recv_sem, pert_send, pert_recv, back_send, back_recv, local_sem,
):
    f32, bf16 = jnp.float32, jnp.bfloat16
    me, lev = lax.axis_index("pts"), lax.axis_index("lev")
    here = {"y": me // 16, "x": (me // 4) % 4, "z": me % 4}
    my_slot = (me * N_LEV + lev) % SLOTS
    chip, core = lev // 2, lev % 2

    def place(at):
        return at["y"] * 16 + at["x"] * 4 + at["z"]

    def moved(axis, step):
        at = dict(here)
        at[axis] = (at[axis] + step) % SIZE[axis]
        return place(at)

    local_copies = [
        pltpu.make_async_copy(horiz, tiles, local_sem.at[0]),
        pltpu.make_async_copy(gradient, grad, local_sem.at[1]),
        pltpu.make_async_copy(vert, vert_raw, local_sem.at[2]),
        pltpu.make_async_copy(pert, pert_raw.at[chip, core, REACH], local_sem.at[3]),
        pltpu.make_async_copy(
            members.at[:, here["y"], here["x"] // 2, here["x"] % 2, here["z"] // 2, here["z"] % 2],
            own,
            local_sem.at[4],
        ),
    ]

    barrier = pltpu.get_barrier_semaphore()
    line = [("x", 1), ("x", 2), ("x", 3), ("z", 1), ("z", 2), ("z", 3), ("y", 1)]
    for axis, step in line:
        pl.semaphore_signal(barrier, inc=1, device_id={"pts": moved(axis, step)}, device_id_type=MESH)
    near = [((me + o + N_PTS) % N_PTS, (lev + r) % N_LEV) for o, r in NEAR]
    for to in near:
        pl.semaphore_signal(barrier, inc=1, device_id=to, device_id_type=MESH)
    for copy in local_copies:
        copy.start()
    pl.semaphore_wait(barrier, len(line) + len(near))

    def pert_copy(i, source, there, to):
        return pltpu.make_async_remote_copy(
            src_ref=source,
            dst_ref=there,
            send_sem=pert_send.at[i],
            recv_sem=pert_recv.at[i],
            device_id=to,
            device_id_type=MESH,
        )

    pert_along = [
        pert_copy(i, pert, pert_raw.at[chip, core, REACH - o], {"pts": (me + o + N_PTS) % N_PTS})
        for i, o in enumerate((1, -1, 2, -2))
    ]
    pert_across = pert_copy(4, pert_raw.at[chip, core], pert_raw.at[chip, core], {"lev": (lev + 2) % N_LEV})
    pert_beside = pert_copy(5, pert_raw.at[:, core], pert_raw.at[:, core], {"lev": lev + 1 - 2 * core})

    hops = (hop1, hop2, hop3)
    held = {}
    sent = []

    def begin(u):
        k, a, b = UNITS[u]
        for part, (low, high) in enumerate(PARTS):
            base = members.at[
                k, :, :, (here["x"] + a) % 2, :, (here["z"] + b) % 2, pl.ds(low, high - low)
            ]
            held[u, part] = [({}, base, NAMES, None)]

    def settle(entry):
        if entry is not None and not entry[1]:
            entry[0].wait_recv()
            entry[1] = True

    def advance(u, part, stage, tick):
        low, high = PARTS[part]
        axis = ORDERS[(part + u) % 3][stage]
        fresh, slot = [], 0
        for moved_by, ref, left, entry in held[u, part]:
            settle(entry)
            for step in distances(UNITS[u], axis):
                target = (here[axis] + step) % SIZE[axis]
                index = target if axis == "y" else target // 2
                source = ref.at[tuple(index if n == axis else slice(None) for n in left)]
                rest = tuple(n for n in left if n != axis)
                by = {**moved_by, axis: step}
                if step == 0:
                    fresh.append((by, source, rest, entry))
                    continue
                assert slot < (2, 4, 8)[stage]
                there = hops[stage].at[
                    (u, part, slot) + (slice(None),) * len(rest) + (pl.ds(0, high - low),)
                ]
                copy = pltpu.make_async_remote_copy(
                    src_ref=source,
                    dst_ref=there,
                    send_sem=send_sem.at[len(sent)],
                    recv_sem=recv_sem.at[len(sent)],
                    device_id={"pts": moved(axis, step)},
                    device_id_type=MESH,
                )
                copy.start()
                sent.append((tick, copy))
                fresh.append((by, there, rest, [copy, False]))
                slot += 1
        held[u, part] = fresh


    def ready_local():
        for copy in local_copies:
            copy.wait()

    def turn_tiles(low, high):
        def body(i, carry):
            turned = [tiles[i * 4 + j].T for j in range(4)]
            for j in range(4):
                tiles[i * 4 + j] = turned[j]
            return carry

        lax.fori_loop(low // 4, high // 4, body, 0)

    def spread_vert():
        def body(i, carry):
            both = vert_raw[i].astype(f32)
            vert_f[2 * i] = both[:8]
            vert_f[2 * i + 1] = both[8:]
            return carry

        lax.fori_loop(0, TILES // 2, body, 0, unroll=4)

    def mark_owners(low, high):
        lanes = lax.broadcasted_iota(jnp.int32, (8, 128), 1)
        live = live_ref[0]

        def body(t, carry):
            slot = owner_ref[t] % SLOTS
            slot = jnp.where(t < live, slot, -1)
            marks[t] = jnp.where(lanes == slot, 1.0, 0.0).astype(f32)
            return carry

        lax.fori_loop(low, high, body, 0, unroll=8)

    def turn_marks():
        for i in range(TILES // 16):
            block = marks[i * 16:(i + 1) * 16].reshape(128, 128)
            group, at = divmod(i, LAST_GROUP // 16)
            select[group, :, at * 128:(at + 1) * 128] = block.T[:SLOTS].astype(bf16)

    def pert_second():
        for copy in pert_along:
            copy.wait_recv()
        pert_across.start()

    def pert_third():
        pert_across.wait_recv()
        pert_beside.start()

    def spread_pert():
        pert_beside.wait_recv()
        for copy in pert_along + [pert_across, pert_beside]:
            copy.wait_send()
        for o in range(-REACH, REACH + 1):
            for r in range(N_LEV):
                slot = (me + o + N_PTS) % (SLOTS // N_LEV) * N_LEV + r
                pert_f[slot] = pert_raw[r // 2, r % 2, o + REACH].astype(f32)

    def sources(u):
        return [
            {"y": dy, "x": dx, "z": dz}
            for dy in distances(UNITS[u], "y")
            for dx in distances(UNITS[u], "x")
            for dz in distances(UNITS[u], "z")
        ]

    def order_pert(u):
        for i, by in enumerate(sources(u)):
            source = place({n: (here[n] - by[n] + SIZE[n]) % SIZE[n] for n in NAMES})
            p, at = places[u]
            pert_u[p, :, pl.ds(at * 8 + i, 1), :] = pert_f[:, pl.ds(source * 2 + UNITS[u][0], 1), :]

    places = {u: (p, at) for p, units in enumerate(PASSES) for at, u in enumerate(units)}

    def arrange(u):
        row = places[u][1] * 64
        for part, (low, high) in enumerate(PARTS):
            refs = []
            for by in sources(u):
                ref, entry = [(item[1], item[3]) for item in held[u, part] if item[0] == by][0]
                settle(entry)
                if not any(by.values()):
                    ref = own.at[UNITS[u][0], pl.ds(low, high - low)]
                refs.append(ref)

            def body(j, carry, low=low, refs=refs, row=row):
                pair = low + j
                g = grad[pair]
                for i in range(0, len(refs), 2):
                    one = refs[i][j].astype(f32) * g
                    two = refs[i + 1][j].astype(f32) * g
                    scaled[2 * pair, row + i * 8:row + i * 8 + 16, :] = jnp.concatenate([one[:8], two[:8]], 0).astype(bf16)
                    scaled[2 * pair + 1, row + i * 8:row + i * 8 + 16, :] = jnp.concatenate([one[8:], two[8:]], 0).astype(bf16)
                return carry

            lax.fori_loop(0, high - low, body, 0)

    def scores(p, first, size):
        results = []
        held_members = 8 * len(PASSES[p])
        left = [scaled[block_ref[first + i], :8 * held_members] for i in range(size)]
        right = [tiles[first + i] for i in range(size)]
        products = [jnp.dot(left[i], right[i], preferred_element_type=f32) for i in range(size)]
        for i in range(size):
            weight = pert_u[p, owner_ref[first + i] % SLOTS, :held_members]
            results.append(jnp.sum(products[i].reshape(held_members, 8, 128) * weight[:, None, :], axis=0))
        return results

    def work(p, low, high):
        def body(i, carry):
            first = i * GROUP
            results = scores(p, first, GROUP)
            if p > 0:
                before = [total[first + j] for j in range(GROUP)]
                results = [results[j] + before[j] for j in range(GROUP)]
            for j in range(GROUP):
                total[first + j] = results[j]
            return carry

        lax.fori_loop(low, high, body, 0)

    def work_last():
        def body(i, carry):
            first = i * LAST_GROUP
            results = scores(len(PASSES) - 1, first, LAST_GROUP)
            results = [(results[j] + total[first + j]) * vert_f[first + j] for j in range(LAST_GROUP)]
            value = jnp.concatenate(results, axis=0)
            high = value.astype(bf16)
            low = (value - high.astype(f32)).astype(bf16)
            chosen = select[i]
            carry = carry + jnp.dot(chosen, high, preferred_element_type=f32)
            return carry + jnp.dot(chosen, low, preferred_element_type=f32)

        return lax.fori_loop(0, TILES // LAST_GROUP, body, jnp.zeros((SLOTS, 128), f32))

    last = len(UNITS) - 1
    turns = [functools.partial(turn_tiles, i, i + 32) for i in range(0, TILES, 32)]
    jobs = [ready_local] + turns[:2] + [pert_second] + turns[2:7] + [pert_third] + turns[7:]
    jobs += [spread_vert]
    jobs += [functools.partial(mark_owners, i, i + 128) for i in range(0, TILES, 128)]
    jobs += [turn_marks, spread_pert]
    jobs += [functools.partial(order_pert, u) for u in range(len(UNITS))]

    def next_job():
        if jobs:
            jobs.pop(0)()

    pending = 0
    for tick in range(last + 1 + 3 * LAG):
        if tick <= last:
            begin(tick)
        done = tick - 3 * LAG
        if done == 0:
            while jobs:
                next_job()
        if 0 <= done < last:
            jobs.append(functools.partial(arrange, done))
            p, at = places[done]
            if at == len(PASSES[p]) - 1:
                jobs += [functools.partial(work, p, i, i + 1) for i in range(TILES // GROUP)]
        for part in range(len(PARTS)):
            for stage in (2, 1, 0):
                u = tick - stage * LAG
                if 0 <= u <= last:
                    advance(u, part, stage, tick)
                    if tick > 0:
                        next_job()
        if tick == 0:
            for copy in pert_along:
                copy.start()
        if tick >= FLUSH:
            while jobs:
                next_job()
        while pending < len(sent) and sent[pending][0] <= tick - 2:
            sent[pending][1].wait_send()
            pending += 1
    arrange(last)
    sums = work_last()
    for s in range(SLOTS):
        rows[s] = sums[s:s + 1]
    back = []
    for i, to in enumerate(near):
        back.append(
            pltpu.make_async_remote_copy(
                src_ref=rows.at[(to[0] * N_LEV + to[1]) % SLOTS],
                dst_ref=arrived.at[i],
                send_sem=back_send.at[i],
                recv_sem=back_recv.at[i],
                device_id=to,
                device_id_type=MESH,
            )
        )
    for copy in back:
        copy.start()
    for copy in back:
        copy.wait_recv()
    whole = rows[my_slot]
    for i in range(len(NEAR)):
        whole = whole + arrived[i]
    out_ref[...] = whole
    for copy in back:
        copy.wait_send()
    for tick, copy in sent[pending:]:
        copy.wait_send()


def local(
    members,
    gradient,
    horiz_loc,
    vert_loc,
    tile_block,
    tile_obs,
    tile_live,
    obs_pert,
    innovation,
    obs_error,
    obs_count,
):
    f32, bf16 = jnp.float32, jnp.bfloat16
    side = 128
    held, levels, columns = members.shape
    moving = members.reshape(held, levels, columns // side, side).transpose(0, 2, 1, 3)
    moving = moving.reshape(held, 2, 2, 2, 2, 2, 32, 16, side)
    slopes = gradient.reshape(levels, 64, side).transpose(1, 0, 2).reshape(32, 16, side)
    vertical = vert_loc.reshape(TILES // 2, 16, side)
    units, parts, count, close = len(UNITS), len(PARTS), moves(), len(NEAR)
    anywhere = pl.BlockSpec(memory_space=pl.ANY)
    scalar = pl.BlockSpec(memory_space=pltpu.SMEM)
    dma = pltpu.SemaphoreType.DMA
    raw_sum = pl.pallas_call(
        kernel,
        name="efsoi",
        out_shape=jax.ShapeDtypeStruct((1, side), f32),
        in_specs=[anywhere] * 4 + [scalar] * 3 + [anywhere],
        out_specs=pl.BlockSpec(memory_space=pltpu.VMEM),
        scratch_shapes=[
            pltpu.VMEM((units, parts, 2, 2, 2, WIDEST, 16, side), bf16),
            pltpu.VMEM((units, parts, 4, 2, WIDEST, 16, side), bf16),
            pltpu.VMEM((units, parts, 8, WIDEST, 16, side), bf16),
            pltpu.VMEM((2, 32, 16, side), bf16),
            pltpu.VMEM((32, 16, side), f32),
            pltpu.VMEM((TILES, side, side), bf16),
            pltpu.VMEM((TILES // 2, 16, side), bf16),
            pltpu.VMEM((TILES, 8, side), f32),
            pltpu.VMEM((64, WIDTH * 64, side), bf16),
            pltpu.VMEM((TILES, 8, side), f32),
            pltpu.VMEM((2, 2, 2 * REACH + 1, 64, side), bf16),
            pltpu.VMEM((SLOTS, 64, side), f32),
            pltpu.VMEM((len(PASSES), SLOTS, WIDTH * 8, side), f32),
            pltpu.VMEM((TILES, 8, side), f32),
            pltpu.VMEM((TILES // LAST_GROUP, SLOTS, LAST_GROUP * 8), bf16),
            pltpu.VMEM((SLOTS, 1, side), f32),
            pltpu.VMEM((close, 1, side), f32),
            dma((count,)),
            dma((count,)),
            dma((6,)),
            dma((6,)),
            dma((close,)),
            dma((close,)),
            dma((5,)),
        ],
        compiler_params=pltpu.CompilerParams(
            collective_id=0, has_side_effects=True, vmem_limit_bytes=56 << 20
        ),
        cost_estimate=pl.CostEstimate(
            flops=2 * TILES * 512 * side * side, bytes_accessed=32 << 20, transcendentals=0
        ),
    )(moving, slopes, horiz_loc, vertical, tile_block, tile_obs, tile_live, obs_pert)
    sensitivity = raw_sum.reshape(side) / (64 - 1)
    observed = jnp.arange(side, dtype=jnp.int32) < obs_count[0]
    sensitivity = jnp.where(observed, sensitivity, jnp.zeros_like(sensitivity))
    impact = innovation * sensitivity / obs_error
    return (sensitivity, impact)


def solution(mesh):
    both = ("pts", "lev")
    placed = (
        P("pts", "lev", None),
        P("lev", "pts"),
        P(both, None, None),
        P(both, None, None),
        P(both),
        P(both),
        P(both),
        P(None, both),
        P(both),
        P(both),
        P(both),
    )
    return jax.shard_map(
        local,
        mesh=mesh,
        in_specs=placed,
        out_specs=(P(both), P(both)),
        check_vma=False,
    )
```
